256 devices in a mesh: sp: 64 (over z, y, core), dp: 4 (over x).
Axes of the slice: x: 4, y: 4, z: 8, core: 2. Of those that a mesh axis runs over, the one named last changes fastest.
Arguments:
- queries: bfloat16 [32768, 8192], P(('dp', 'sp')), parts along dimension 0, may hold values from -60 to 60
- key_heads: bfloat16 [32768, 1024], P(('dp', 'sp')), parts along dimension 0, may hold values from -6 to 6
- value_heads: bfloat16 [32768, 1024], P(('dp', 'sp')), parts along dimension 0, may hold values from -6 to 6
- out_grad: bfloat16 [32768, 8192], P(('dp', 'sp')), parts along dimension 0, may hold values from -6 to 6
- segment_ids: int32 [32768], P(('dp', 'sp')), parts along dimension 0, may hold values from 0 to 31, never falling along the last dimension, each value on 1 to 512 neighbouring positions
Outputs:
- d_query: bfloat16 [32768, 8192], P(('dp', 'sp')), parts along dimension 0
- d_key: bfloat16 [32768, 1024], P(('dp', 'sp')), parts along dimension 0
- d_value: bfloat16 [32768, 1024], P(('dp', 'sp')), parts along dimension 0
The draws below stay inside these ranges and needn't reach their ends.
There are 4 independent parts, one for each index of `dp`. The reference program is written for one: setup_inputs(seed, part) draws one part's arguments, and reference() takes and returns one part's arrays. A program takes and returns all parts, laid end to end along the dimension named above; each array names one. Nothing has to cross between parts.
Inputs may be any that keep to these rules, and one draw needn't show every extreme that they name: `segment_ids`: documents are runs of consecutive tokens with rising ids, each of at most 512 tokens; one has exactly 512.
All inputs are finite; a program needn't handle non-finite values.
Results may differ from the reference program's by a relative error of at most 0.0065.
Values may be sent and summed in bfloat16 or wider, within the bound.
No kernel may reach another device: no remote copies, remote signals or barrier semaphores. Data moves between devices by JAX's collectives and lax.ppermute only.
A program may use at most 192 MiB of HBM per device.

```python
import math
import jax
import jax.numpy as jnp
import numpy as np
from jax import lax

HEADS = 64
KV_HEADS = 8
HEAD_DIM = 128
GROUP = 8
MOST = 512
SEQ = 8192
DOCS = 32


def paired_keys(key):
    raw = jax.random.truncated_normal(key, -4.0, 4.0, (SEQ // 2, 2, KV_HEADS * HEAD_DIM), jnp.float32)
    partner = raw[:, 0]
    return jnp.stack([partner, raw[:, 1]], axis=1).reshape(SEQ, KV_HEADS * HEAD_DIM)


def draw_key_heads(key, part):
    shared = paired_keys(key)
    return shared.astype(jnp.bfloat16)


def draw_queries(key, part):
    key = jax.random.fold_in(key, 3)
    drawn = jax.random.truncated_normal(key, -4.0, 4.0, (SEQ, KV_HEADS, GROUP, HEAD_DIM), jnp.float32)
    return drawn.reshape(SEQ, HEADS * HEAD_DIM).astype(jnp.bfloat16)


def level_of(stream_key, shape, shards, smallest, top_value):
    def one(axis_at, parts):
        draws = jax.random.uniform(jax.random.fold_in(jax.random.fold_in(stream_key, 6), axis_at), (parts,), jnp.float32, smallest / len(shards), top_value / len(shards))
        return jnp.repeat(jnp.exp(draws), shape[axis_at] // parts).reshape((-1,) + (1,) * (len(shape) - axis_at - 1))

    loudness = one(*shards[0])
    for cut in shards[1:]:
        loudness = loudness * one(*cut)
    return loudness


def profile(number_of, total, most, lean):
    portions = [(1 << 20) // math.isqrt(grade ** lean) + 1 for grade in range(2, number_of + 1)]
    rest, given = total - most - (number_of - 1), [1] * (number_of - 1)
    while rest > 0:
        free = [i for i in range(number_of - 1) if given[i] < most]
        whole, left = sum([portions[i] for i in free]), rest
        for i in free:
            more = min(most - given[i], max(1, left * portions[i] // whole), rest)
            given[i] = given[i] + more
            rest = rest - more
    return np.array([most] + given)


def ragged_sizes(own_key, number_of, total, reach, lean):
    if number_of == 2:
        one = jax.random.randint(own_key, (), max(1, total - reach), min(reach, total - 1) + 1)
        return jnp.stack([one, total - one])
    lengths = jnp.asarray(profile(number_of, total, reach, lean), jnp.int32)
    twos = (number_of - 1) // 2
    source_of, receiver = lengths[1:1 + 2 * twos:2], lengths[2:2 + 2 * twos:2]
    slack = jnp.minimum(source_of - 1, reach - receiver)
    shifted = jax.random.randint(jax.random.fold_in(own_key, 1), (twos,), 0, 1 << 20) % (slack + 1)
    lengths = lengths.at[1:1 + 2 * twos:2].set(source_of - shifted).at[2:2 + 2 * twos:2].set(receiver + shifted)
    return lengths[jax.random.permutation(jax.random.fold_in(own_key, 2), number_of)]


def bell_draw(stream_key, dims, spread, most, pieces=(), kind=jnp.bfloat16):
    array = spread * jax.random.normal(stream_key, dims, jnp.float32)
    if pieces:
        array = array * level_of(stream_key, dims, pieces, -0.22, 0.18)
    return jnp.clip(array, -most, most).astype(kind)


def setup_inputs(seed: int = 0, part: int = 0) -> dict:
    key_list = jax.random.split(jax.random.key(seed), 6)
    part_keys = jax.random.split(jax.random.fold_in(key_list[5], part), 6)
    queries = draw_queries(jax.random.fold_in(jax.random.fold_in(key_list[5], part), 71), part)
    key_heads = draw_key_heads(jax.random.fold_in(jax.random.fold_in(key_list[5], part), 71), part)
    value_heads = bell_draw(part_keys[2], (SEQ, KV_HEADS * HEAD_DIM), 1.0, 6.0, ((0, 64),))
    out_grad = bell_draw(part_keys[3], (SEQ, HEADS * HEAD_DIM), 1.0, 6.0, ((0, 64),))
    segment_ids = jnp.searchsorted(jnp.cumsum(ragged_sizes(part_keys[4], DOCS, SEQ, MOST, 2)), jnp.arange(SEQ), side="right").astype(jnp.int32)
    return {"queries": queries, "key_heads": key_heads, "value_heads": value_heads, "out_grad": out_grad, "segment_ids": segment_ids}


def reference(queries, key_heads, value_heads, out_grad, segment_ids):
    scale = HEAD_DIM ** -0.5
    block = min(512, SEQ)
    span = MOST + block
    count = SEQ // block
    kv_width = KV_HEADS * HEAD_DIM
    keys_pad = jnp.concatenate([jnp.zeros((MOST, kv_width), jnp.bfloat16), key_heads], axis=0)
    values_pad = jnp.concatenate([jnp.zeros((MOST, kv_width), jnp.bfloat16), value_heads], axis=0)
    ids_pad = jnp.concatenate([jnp.full((MOST,), -1, jnp.int32), segment_ids.astype(jnp.int32)], axis=0)

    def one_block(carry, number):
        key_acc, value_acc = carry
        start = (number * block).astype(jnp.int32)
        q_blk = lax.dynamic_slice_in_dim(queries, start, block, 0).reshape(block, KV_HEADS, GROUP, HEAD_DIM).astype(jnp.float32)
        g_blk = lax.dynamic_slice_in_dim(out_grad, start, block, 0).reshape(block, KV_HEADS, GROUP, HEAD_DIM).astype(jnp.float32)
        k_win = lax.dynamic_slice_in_dim(keys_pad, start, span, 0).reshape(span, KV_HEADS, HEAD_DIM).astype(jnp.float32)
        v_win = lax.dynamic_slice_in_dim(values_pad, start, span, 0).reshape(span, KV_HEADS, HEAD_DIM).astype(jnp.float32)
        ids_q = lax.dynamic_slice_in_dim(segment_ids.astype(jnp.int32), start, block, 0)
        ids_k = lax.dynamic_slice_in_dim(ids_pad, start, span, 0)
        q_pos = start + jnp.arange(block, dtype=jnp.int32)
        k_pos = start - MOST + jnp.arange(span, dtype=jnp.int32)
        allowed = (ids_q[:, None] == ids_k[None, :]) & (k_pos[None, :] <= q_pos[:, None])
        scores = jnp.einsum("qkgd,jkd->kgqj", q_blk, k_win) * scale
        scores = jnp.where(allowed, scores, -1e30)
        row_max = jnp.max(scores, axis=-1, keepdims=True)
        probs = jnp.exp(scores - row_max)
        probs = probs / jnp.sum(probs, axis=-1, keepdims=True)
        probs_low = lax.optimization_barrier(probs.astype(jnp.bfloat16)).astype(jnp.float32)
        prob_grads = jnp.einsum("qkgd,jkd->kgqj", g_blk, v_win)
        delta = jnp.sum(probs * prob_grads, axis=-1, keepdims=True)
        score_grads = lax.optimization_barrier((probs * (prob_grads - delta)).astype(jnp.bfloat16)).astype(jnp.float32)
        query_grad = jnp.einsum("kgqj,jkd->qkgd", score_grads, k_win) * scale
        key_part = jnp.einsum("kgqj,qkgd->jkd", score_grads, q_blk) * scale
        value_part = jnp.einsum("kgqj,qkgd->jkd", probs_low, g_blk)
        old_key = lax.dynamic_slice_in_dim(key_acc, start, span, 0)
        old_value = lax.dynamic_slice_in_dim(value_acc, start, span, 0)
        key_acc = lax.dynamic_update_slice_in_dim(key_acc, old_key + key_part, start, 0)
        value_acc = lax.dynamic_update_slice_in_dim(value_acc, old_value + value_part, start, 0)
        return (key_acc, value_acc), query_grad.reshape(block, HEADS * HEAD_DIM).astype(jnp.bfloat16)

    zeros_acc = jnp.zeros((SEQ + MOST, KV_HEADS, HEAD_DIM), jnp.float32)
    (key_acc, value_acc), query_blocks = lax.scan(one_block, (zeros_acc, zeros_acc), jnp.arange(count, dtype=jnp.int32))
    d_query = query_blocks.reshape(SEQ, HEADS * HEAD_DIM)
    d_key = key_acc[MOST:].reshape(SEQ, kv_width).astype(jnp.bfloat16)
    d_value = value_acc[MOST:].reshape(SEQ, kv_width).astype(jnp.bfloat16)
    return (d_query, d_key, d_value)
```

```python
import functools

import jax
import jax.numpy as jnp
from jax import lax
from jax.experimental import pallas as pl
from jax.experimental.pallas import tpu as pltpu
from jax.sharding import PartitionSpec as P

D = 128
T = 128
GROUP = 8
NEG = -1e30
CHUNKS = 2
CORE_HEADS = 4
HC = CORE_HEADS // CHUNKS
PAY = HC * 512 + 16
SCALE = D ** -0.5
LOG2E = 1.4426950408889634
NT = (((1,), (1,)), ((), ()))
TN = (((0,), (0,)), ((), ()))
NN = (((1,), (0,)), ((), ()))
F32 = jnp.float32
BF16 = jnp.bfloat16


def rows(start, size, step=128):
    return pl.ds(pl.multiple_of(start, step), size)


def prep_kernel(info, key, value, ids, mine, theirs):
    c = info[0]
    for out, core in ((mine, c), (theirs, 1 - c)):
        for h in range(CORE_HEADS):
            cols = rows((core * CORE_HEADS + h) * D, D)
            out[(2 * h) * T:(2 * h + 1) * T, :] = key[:, cols]
            out[(2 * h + 1) * T:(2 * h + 2) * T, :] = value[:, cols]
        out[2 * CORE_HEADS * T:, :] = jnp.broadcast_to(ids[...].astype(F32), (16, T)).astype(BF16)


def join_kernel(info, mine, other, *outs):
    c = info[0]
    for j, out in enumerate(outs):
        for ht in range(2 * HC):
            src = (j * 2 * HC + ht) * T
            out[rows(ht * 256 + c * T, T), :] = mine[src:src + T, :]
            out[rows(ht * 256 + (1 - c) * T, T), :] = other[src:src + T, :]
        a = mine[2 * CORE_HEADS * T:, :].astype(F32)
        b = other[2 * CORE_HEADS * T:, :].astype(F32)
        row = lax.broadcasted_iota(jnp.int32, (16, T), 0)
        out[HC * 512:, :] = jnp.where(row == c, a, b).astype(BF16)


def main_kernel(info, kvo, kv1, kv2, io, i1, i2, qo, qr, go, gr,
                dqo, dqr, own, out1, out2,
                idrow, nb, bias, kwin, vwin, acc_k, acc_v, qs, gs, ps, ds, dqs):
    c, k = info[0], info[1]

    @pl.when(pl.program_id(0) == 0)
    def _():
        old = jnp.where(k >= 2, i2[0:2, :].astype(F32), -1.0)
        mid = jnp.where(k >= 1, i1[0:2, :].astype(F32), -1.0)
        idrow[0:2, :] = old
        idrow[2:4, :] = mid
        idrow[4:6, :] = io[0:2, :].astype(F32)
        key_at = lax.broadcasted_iota(jnp.int32, (T, T), 0)
        query_at = lax.broadcasted_iota(jnp.int32, (T, T), 1)
        for n in range(2):
            s = c if n == 0 else 1 - c
            mine = idrow[pl.ds(s + 4, 1), :]
            first = jnp.max(jnp.where(lax.broadcasted_iota(jnp.int32, (1, T), 1) == 0, mine, -2.0))
            count = jnp.int32(1)
            for b in range(5):
                keys = idrow[pl.ds(s + b, 1), :]
                same = jnp.transpose(jnp.broadcast_to(keys, (T, T))) == mine
                if b == 4:
                    same = same & (key_at <= query_at)
                else:
                    count = count + (jnp.max(keys) == first).astype(jnp.int32)
                bias[n, b * T:(b + 1) * T, :] = jnp.where(same, 0.0, NEG)
            nb[n] = count

    for at, ref in ((0, kv2), (256, kv1), (512, kvo)):
        kwin[at:at + 256, :] = ref[0:256, :]
        vwin[at:at + 256, :] = ref[256:512, :]
    acc_k[...] = jnp.zeros_like(acc_k)
    acc_v[...] = jnp.zeros_like(acc_v)
    for n, (q, g) in enumerate(((qo, go), (qr, gr))):
        for h in range(GROUP):
            qs[n, h * T:(h + 1) * T, :] = q[:, h * D:(h + 1) * D]
            gs[n, h * T:(h + 1) * T, :] = g[:, h * D:(h + 1) * D]

    def window(n, off, blocks):
        width = blocks * T
        at = rows(off + (5 - blocks) * T, width)
        kw, vw = kwin[at, :], vwin[at, :]
        b1 = bias[n, 640 - width:, :]
        b2 = jnp.concatenate([b1, b1], axis=1)
        for pair in range(GROUP // 2):
            cols = slice(pair * 256, (pair + 1) * 256)
            score = lax.dot_general(kw, qs[n, cols, :], NT, preferred_element_type=F32)
            dp = lax.dot_general(vw, gs[n, cols, :], NT, preferred_element_type=F32)
            score = score * (SCALE * LOG2E) + b2
            e = jnp.exp2(score - jnp.max(score, axis=0, keepdims=True))
            inv = 1.0 / jnp.sum(e, axis=0, keepdims=True)
            delta = jnp.sum(e * dp, axis=0, keepdims=True) * inv
            p = e * inv
            ps[0:width, cols] = p.astype(BF16)
            ds[0:width, cols] = (p * (dp - delta)).astype(BF16)
        dsv = ds[0:width, :]
        acc_v[at, :] += lax.dot_general(ps[0:width, :], gs[n], NN, preferred_element_type=F32)
        acc_k[at, :] += lax.dot_general(dsv, qs[n], NN, preferred_element_type=F32)
        dqs[n] = (lax.dot_general(dsv, kw, TN, preferred_element_type=F32) * SCALE).astype(BF16)

    def half(n, carry):
        off = jnp.where(n == 0, c, 1 - c) * T
        for blocks in range(1, 6):
            @pl.when(nb[n] == blocks)
            def _():
                window(n, off, blocks)
        return carry

    lax.fori_loop(0, 2, half, 0)

    for n, out in enumerate((dqo, dqr)):
        for h in range(GROUP):
            out[:, h * D:(h + 1) * D] = dqs[n, h * T:(h + 1) * T, :]
    for at, ref in ((0, out2), (256, out1), (512, own)):
        ref[0:256, :] = (acc_k[at:at + 256, :] * SCALE).astype(ref.dtype)
        ref[256:512, :] = acc_v[at:at + 256, :].astype(ref.dtype)


def sum_kernel(info, own, b1, b2, mine, theirs):
    c = info[0]
    for out, core in ((mine, c), (theirs, 1 - c)):
        for ht in range(2 * HC):
            at = rows(ht * 256 + core * T, T)
            out[ht * T:(ht + 1) * T, :] = (
                own[at, :] + b1[at, :].astype(F32) + b2[at, :].astype(F32)).astype(BF16)


def last_kernel(info, *refs):
    c = info[0]
    mine, other, (key, value) = refs[:CHUNKS], refs[CHUNKS:2 * CHUNKS], refs[2 * CHUNKS:]
    for part, core in ((mine, c), (other, 1 - c)):
        for j in range(CHUNKS):
            for h in range(HC):
                cols = rows((core * CORE_HEADS + j * HC + h) * D, D)
                key[:, cols] = part[j][(2 * h) * T:(2 * h + 1) * T, :]
                value[:, cols] = part[j][(2 * h + 1) * T:(2 * h + 2) * T, :]


def shape(*dims, dtype=BF16):
    return jax.ShapeDtypeStruct(dims, dtype)


SMEM = pl.BlockSpec(memory_space=pltpu.SMEM)
VMEM = pl.BlockSpec(memory_space=pltpu.VMEM)


def simple(kernel, outs, count, flops=0):
    return pl.pallas_call(
        kernel,
        out_shape=outs,
        in_specs=[SMEM] + [VMEM] * count,
        out_specs=tuple(VMEM for _ in outs),
        compiler_params=pltpu.CompilerParams(vmem_limit_bytes=16 * 1024 * 1024),
    )


def main_call(chunk, info, payload, r1, r2, queries, q_other, out_grad, g_other):
    base = chunk * HC
    kv = pl.BlockSpec((512, T), lambda h, info: (h, 0))
    ids = pl.BlockSpec((16, T), lambda h, info: (HC * 512 // 16, 0))
    own = pl.BlockSpec((T, GROUP * D), lambda h, info: (0, info[0] * CORE_HEADS + base + h))
    other = pl.BlockSpec((T, GROUP * D), lambda h, info: (0, base + h))
    part = pl.BlockSpec((T, GROUP * D), lambda h, info: (0, h))
    return pl.pallas_call(
        main_kernel,
        grid_spec=pltpu.PrefetchScalarGridSpec(
            num_scalar_prefetch=1,
            grid=(HC,),
            in_specs=[kv, kv, kv, ids, ids, ids, own, other, own, other],
            out_specs=[part, part, kv, kv, kv],
            scratch_shapes=[
                pltpu.VMEM((8, T), F32),
                pltpu.SMEM((2,), jnp.int32),
                pltpu.VMEM((2, 640, T), F32),
                pltpu.VMEM((768, D), BF16),
                pltpu.VMEM((768, D), BF16),
                pltpu.VMEM((768, D), F32),
                pltpu.VMEM((768, D), F32),
                pltpu.VMEM((2, 1024, D), BF16),
                pltpu.VMEM((2, 1024, D), BF16),
                pltpu.VMEM((640, 1024), BF16),
                pltpu.VMEM((640, 1024), BF16),
                pltpu.VMEM((2, 1024, D), BF16),
            ],
        ),
        out_shape=[
            shape(T, HC * 1024),
            shape(T, HC * 1024),
            shape(HC * 512, T, dtype=F32),
            shape(HC * 512, T),
            shape(HC * 512, T),
        ],
        compiler_params=pltpu.CompilerParams(
            dimension_semantics=("arbitrary",), vmem_limit_bytes=48 * 1024 * 1024),
        cost_estimate=pl.CostEstimate(
            flops=HC * 2 * 640 * 1024 * 128 * 10 * 2, bytes_accessed=HC * 3 * 1024 * 1024,
            transcendentals=HC * 2 * 640 * 1024),
    )(info, payload, r1, r2, payload, r1, r2, queries, q_other, out_grad, g_other)


def body(queries, key_heads, value_heads, out_grad, segment_ids):
    devices = lax.axis_size("sp")
    me = lax.axis_index("sp")
    c, k = me % 2, me // 2
    info = jnp.stack([c, k]).astype(jnp.int32)
    swap = [(i, i ^ 1) for i in range(devices)]

    def ring(by):
        return [(i, (i + by) % devices) for i in range(devices)]

    def send(x, perm):
        return lax.ppermute(x, "sp", perm)

    side = shape(2 * CORE_HEADS * T + 16, T)
    mine, theirs = simple(prep_kernel, (side, side), 3)(
        info, key_heads, value_heads, segment_ids.reshape(1, T))
    other = send(theirs, swap)
    payloads = simple(join_kernel, (shape(PAY, T),) * CHUNKS, 2)(info, mine, other)
    came = [(send(p, ring(2)), send(p, ring(4))) for p in payloads]
    width = CORE_HEADS * GROUP * D
    start = (1 - c) * width
    q_other = send(lax.dynamic_slice(queries, (0, start), (T, width)), swap)
    g_other = send(lax.dynamic_slice(out_grad, (0, start), (T, width)), swap)

    dq_own, dq_other, kv_mine, kv_other = [], [], [], []
    for j in range(CHUNKS):
        dqo, dqr, own, out1, out2 = main_call(
            j, info, payloads[j], *came[j], queries, q_other, out_grad, g_other)
        dq_own.append(dqo)
        dq_other.append(send(dqr, swap))
        b2 = send(out2, ring(-4))
        b1 = send(out1, ring(-2))
        half = shape(2 * HC * T, T)
        a, b = simple(sum_kernel, (half, half), 3)(info, own, b1, b2)
        kv_mine.append(a)
        kv_other.append(send(b, swap))

    left = jnp.concatenate(dq_own, axis=1)
    right = jnp.concatenate(dq_other, axis=1)
    d_query = jnp.where(
        c == 0, jnp.concatenate([left, right], axis=1), jnp.concatenate([right, left], axis=1))
    out = shape(T, 2 * CORE_HEADS * D)
    d_key, d_value = simple(last_kernel, (out, out), 2 * CHUNKS)(info, *kv_mine, *kv_other)
    return (d_query, d_key, d_value)


def solution(mesh):
    row = P(("dp", "sp"), None)
    return jax.shard_map(
        body,
        mesh=mesh,
        in_specs=(row, row, row, row, P(("dp", "sp"))),
        out_specs=(row, row, row),
        check_vma=False,
    )
```

```python
import functools

import jax
import jax.numpy as jnp
from jax import lax
from jax.experimental import pallas as pl
from jax.experimental.pallas import tpu as pltpu
from jax.sharding import PartitionSpec as P

D = 128
T = 128
GROUP = 8
NEG = -1e30
CHUNKS = 2
CORE_HEADS = 4
HC = CORE_HEADS // CHUNKS
PAY = HC * 512 + 16
SMALL = 16 * 1024 * 1024
ROWS = 128
HALF = 512
SCALE = D ** -0.5
LOG2E = 1.4426950408889634
NT = (((1,), (1,)), ((), ()))
TN = (((0,), (0,)), ((), ()))
NN = (((1,), (0,)), ((), ()))
F32 = jnp.float32
BF16 = jnp.bfloat16


def rows(start, size, step=128):
    return pl.ds(pl.multiple_of(start, step), size)


def prep_kernel(info, key_in, value_in, ids_in, mine, theirs, key, value, ids, sems):
    c = info[0]
    pairs = ((key_in, key), (value_in, value), (ids_in, ids))
    copies = [pltpu.make_async_copy(a, b, sems.at[i]) for i, (a, b) in enumerate(pairs)]
    for copy in copies:
        copy.start()
    for copy in copies:
        copy.wait()
    for out, core in ((theirs, 1 - c), (mine, c)):
        for h in range(CORE_HEADS):
            cols = rows((core * CORE_HEADS + h) * D, D)
            out[(2 * h) * T:(2 * h + 1) * T, :] = key[:, cols]
            out[(2 * h + 1) * T:(2 * h + 2) * T, :] = value[:, cols]
        out[2 * CORE_HEADS * T:, :] = jnp.broadcast_to(ids[...].astype(F32), (16, T)).astype(BF16)


def join_kernel(info, mine, other, *outs):
    c = info[0]
    for j, out in enumerate(outs):
        for ht in range(2 * HC):
            src = (j * 2 * HC + ht) * T
            out[rows(ht * 256 + c * T, T), :] = mine[src:src + T, :]
            out[rows(ht * 256 + (1 - c) * T, T), :] = other[src:src + T, :]
        a = mine[2 * CORE_HEADS * T:, :].astype(F32)
        b = other[2 * CORE_HEADS * T:, :].astype(F32)
        row = lax.broadcasted_iota(jnp.int32, (16, T), 0)
        out[HC * 512:, :] = jnp.where(row == c, a, b).astype(BF16)


def main_kernel(chunk, info, kvo, kv1, kv2, qo, qr, go, gr, *refs):
    base = chunk * HC
    refs = refs[0 if chunk == 0 else 2:]
    main_steps(base, info, kvo, kv1, kv2, qo, qr, go, gr, *refs)


def main_steps(base, info, kvo, kv1, kv2, qo, qr, go, gr,
                dqo, dqr, own, out1, out2,
                idrow, nb, bias, kwin, vwin, acc_k, acc_v, qs, gs, ps, ds, dqs, es, dps):
    c, k = info[0], info[1]
    ids = slice(HC * 512, HC * 512 + 2)
    idrow[0:2, :] = jnp.where(k >= 2, kv2[ids, :].astype(F32), -1.0)
    idrow[2:4, :] = jnp.where(k >= 1, kv1[ids, :].astype(F32), -1.0)
    idrow[4:6, :] = kvo[ids, :].astype(F32)
    key_at = lax.broadcasted_iota(jnp.int32, (T, T), 0)
    query_at = lax.broadcasted_iota(jnp.int32, (T, T), 1)
    for n in range(2):
        s = c if n == 0 else 1 - c
        mine = idrow[pl.ds(s + 4, 1), :]
        first = jnp.max(jnp.where(lax.broadcasted_iota(jnp.int32, (1, T), 1) == 0, mine, -2.0))
        count = jnp.int32(1)
        for b in range(5):
            keys = idrow[pl.ds(s + b, 1), :]
            same = jnp.transpose(jnp.broadcast_to(keys, (T, T))) == mine
            if b == 4:
                same = same & (key_at <= query_at)
            else:
                count = count + (jnp.max(keys) == first).astype(jnp.int32)
            bias[n, b * T:(b + 1) * T, :] = jnp.where(same, 0.0, NEG)
        nb[n] = count

    def window(n, off, blocks):
        width = blocks * T
        at = rows(off + (5 - blocks) * T, width)
        kw, vw = kwin[at, :], vwin[at, :]
        b1 = bias[n, 640 - width:, :]
        b2 = jnp.concatenate([b1, b1], axis=1)
        for pair in range(GROUP // 2):
            cols = slice(pair * 256, (pair + 1) * 256)
            score = lax.dot_general(kw, qs[cols, :], NT, preferred_element_type=F32)
            dp = lax.dot_general(vw, gs[cols, :], NT, preferred_element_type=F32)
            stats = []
            for b in range(0, width, ROWS):
                x = score[b:b + ROWS] * (SCALE * LOG2E) + b2[b:b + ROWS]
                x = x.reshape(ROWS // 8, 8, 256)
                y = dp[b:b + ROWS].reshape(ROWS // 8, 8, 256)
                top = jnp.max(x, axis=0)
                e = jnp.exp2(x - top)
                stats.append((top, jnp.sum(e, axis=0), jnp.sum(e * y, axis=0)))
                es[pair % 2, b:b + ROWS, :] = e.reshape(ROWS, 256)
                dps[pair % 2, b:b + ROWS, :] = dp[b:b + ROWS]
            top = stats[0][0]
            for t, _, _ in stats[1:]:
                top = jnp.maximum(top, t)
            top = jnp.max(top, axis=0, keepdims=True)
            fs = [jnp.exp2(t - top) for t, _, _ in stats]
            total = sum(f * l for f, (_, l, _) in zip(fs, stats))
            inv = 1.0 / jnp.sum(total, axis=0, keepdims=True)
            total = sum(f * d for f, (_, _, d) in zip(fs, stats))
            delta = jnp.sum(total, axis=0, keepdims=True) * inv
            for b, f in zip(range(0, width, ROWS), fs):
                at_b = slice(b, b + ROWS)
                p = es[pair % 2, at_b, :].reshape(ROWS // 8, 8, 256) * (f * inv)
                y = dps[pair % 2, at_b, :].reshape(ROWS // 8, 8, 256)
                ps[at_b, cols] = p.reshape(ROWS, 256).astype(BF16)
                ds[at_b, cols] = (p * (y - delta)).reshape(ROWS, 256).astype(BF16)
            done = (pair + 1) * 256
            if done % HALF == 0:
                part = slice(done - HALF, done)
                dsv = ds[0:width, part]
                acc_v[at, :] += lax.dot_general(
                    ps[0:width, part], gs[part, :], NN, preferred_element_type=F32)
                acc_k[at, :] += lax.dot_general(
                    dsv, qs[part, :], NN, preferred_element_type=F32)
                dqs[part, :] = (lax.dot_general(
                    dsv, kw, TN, preferred_element_type=F32) * SCALE).astype(BF16)

    def one_head(h, carry):
        for at, ref in ((0, kv2), (256, kv1), (512, kvo)):
            kwin[at:at + 256, :] = ref[rows(h * 512, 256), :]
            vwin[at:at + 256, :] = ref[rows(h * 512 + 256, 256), :]
        acc_k[...] = jnp.zeros_like(acc_k)
        acc_v[...] = jnp.zeros_like(acc_v)
        col = (base + h) * (GROUP * D)
        wide = (c * CORE_HEADS + base + h) * (GROUP * D)

        def half(n, carry):
            for m, (q, g, at_q) in enumerate(((qo, go, col), (qr, gr, wide))):
                @pl.when(n == m)
                def _():
                    for i in range(GROUP):
                        to = slice(i * T, (i + 1) * T)
                        qs[to, :] = q[:, rows(at_q + i * D, D)]
                        gs[to, :] = g[:, rows(at_q + i * D, D)]
            off = jnp.where(n == 0, c, 1 - c) * T
            for blocks in range(1, 6):
                @pl.when(nb[n] == blocks)
                def _():
                    window(n, off, blocks)
            for m, out in enumerate((dqo, dqr)):
                @pl.when(n == m)
                def _():
                    for i in range(GROUP):
                        out[:, rows(col + i * D, D)] = dqs[i * T:(i + 1) * T, :]
            return carry

        lax.fori_loop(0, 2, half, 0)
        for at, ref in ((0, out2), (256, out1), (512, own)):
            ref[rows(h * 512, 256), :] = (acc_k[at:at + 256, :] * SCALE).astype(ref.dtype)
            ref[rows(h * 512 + 256, 256), :] = acc_v[at:at + 256, :].astype(ref.dtype)
        return carry

    lax.fori_loop(0, HC, one_head, 0)


def stage_kernel(info, query, grad, query_out, grad_out):
    start = info[0] * (CORE_HEADS * GROUP * D)
    for i in range(0, CORE_HEADS * GROUP * D, D):
        query_out[:, i:i + D] = query[:, rows(start + i, D)]
        grad_out[:, i:i + D] = grad[:, rows(start + i, D)]


def place_kernel(info, mine, other, out, token):
    c = info[0]
    width = CORE_HEADS * GROUP * D
    for part, core in ((mine, c), (other, 1 - c)):
        for i in range(0, width, D):
            out[:, rows(core * width + i, D)] = part[:, i:i + D]
    token[...] = jnp.zeros_like(token)


def sum_kernel(info, own, b1, b2, after, mine, theirs):
    c = info[0]
    for out, core in ((mine, c), (theirs, 1 - c)):
        for ht in range(2 * HC):
            at = rows(ht * 256 + core * T, T)
            out[ht * T:(ht + 1) * T, :] = (
                own[at, :] + b1[at, :].astype(F32) + b2[at, :].astype(F32)).astype(BF16)


def last_kernel(info, *refs):
    c = info[0]
    mine, other, (key, value) = refs[:CHUNKS], refs[CHUNKS:2 * CHUNKS], refs[2 * CHUNKS:]
    for part, core in ((mine, c), (other, 1 - c)):
        for j in range(CHUNKS):
            for h in range(HC):
                cols = rows((core * CORE_HEADS + j * HC + h) * D, D)
                key[:, cols] = part[j][(2 * h) * T:(2 * h + 1) * T, :]
                value[:, cols] = part[j][(2 * h + 1) * T:(2 * h + 2) * T, :]


def shape(*dims, dtype=BF16):
    return jax.ShapeDtypeStruct(dims, dtype)


SMEM = pl.BlockSpec(memory_space=pltpu.SMEM)
ANY = pl.BlockSpec(memory_space=pl.ANY)
HBM = pl.BlockSpec(memory_space=pltpu.HBM)
FREE = pl.CostEstimate(flops=0, bytes_accessed=0, transcendentals=0)
LONG = pl.CostEstimate(flops=10 ** 11, bytes_accessed=10 ** 8, transcendentals=0)
VMEM = pl.BlockSpec(memory_space=pltpu.VMEM)


def simple(kernel, outs, count, flops=0):
    return pl.pallas_call(
        kernel,
        out_shape=outs,
        in_specs=[SMEM] + [VMEM] * count,
        out_specs=tuple(VMEM for _ in outs),
        compiler_params=pltpu.CompilerParams(vmem_limit_bytes=SMALL),
            cost_estimate=FREE,
    )


def main_call(chunk, info, payload, r1, r2, qo, qr, go, gr, *dq):
    return pl.pallas_call(
        functools.partial(main_kernel, chunk),
        in_specs=[SMEM] + [VMEM] * 7 + [ANY] * len(dq),
        input_output_aliases={8: 0, 9: 1} if dq else {},
        out_specs=[VMEM] * 5,
        scratch_shapes=[
            pltpu.VMEM((8, T), F32),
            pltpu.SMEM((2,), jnp.int32),
            pltpu.VMEM((2, 640, T), F32),
            pltpu.VMEM((768, D), BF16),
            pltpu.VMEM((768, D), BF16),
            pltpu.VMEM((768, D), F32),
            pltpu.VMEM((768, D), F32),
            pltpu.VMEM((1024, D), BF16),
            pltpu.VMEM((1024, D), BF16),
            pltpu.VMEM((640, 1024), BF16),
            pltpu.VMEM((640, 1024), BF16),
            pltpu.VMEM((1024, D), BF16),
            pltpu.VMEM((2, 640, 256), F32),
            pltpu.VMEM((2, 640, 256), F32),
        ],
        out_shape=[
            shape(T, CORE_HEADS * 1024),
            shape(T, CORE_HEADS * 1024),
            shape(HC * 512, T, dtype=F32),
            shape(HC * 512, T),
            shape(HC * 512, T),
        ],
        compiler_params=pltpu.CompilerParams(vmem_limit_bytes=24 * 1024 * 1024),
        cost_estimate=LONG,
    )(info, payload, r1, r2, qo, qr, go, gr, *dq)


def body(queries, key_heads, value_heads, out_grad, segment_ids):
    devices = lax.axis_size("sp")
    me = lax.axis_index("sp")
    c, k = me % 2, me // 2
    info = jnp.stack([c, k]).astype(jnp.int32)
    swap = [(i, i ^ 1) for i in range(devices)]

    def ring(by):
        return [(i, (i + by) % devices) for i in range(devices)]

    def send(x, perm):
        return lax.ppermute(x, "sp", perm)

    side = shape(2 * CORE_HEADS * T + 16, T)
    kv_in = pltpu.VMEM((T, 2 * CORE_HEADS * D), BF16)
    mine, theirs = pl.pallas_call(
        prep_kernel,
        out_shape=(side, side),
        in_specs=[SMEM, HBM, HBM, HBM],
        out_specs=(VMEM, VMEM),
        scratch_shapes=[
            kv_in, kv_in, pltpu.VMEM((1, T), jnp.int32), pltpu.SemaphoreType.DMA((3,))],
        compiler_params=pltpu.CompilerParams(vmem_limit_bytes=SMALL),
        cost_estimate=FREE,
    )(info, key_heads, value_heads, segment_ids.reshape(1, T))
    other = send(theirs, swap)
    q_late, g_late, other = lax.optimization_barrier((queries, out_grad, other))
    q_other, g_other = send(q_late, swap), send(g_late, swap)
    payloads = simple(join_kernel, (shape(PAY, T),) * CHUNKS, 2)(info, mine, other)
    near, far = send(payloads[0], ring(2)), send(payloads[0], ring(4))
    half = shape(T, CORE_HEADS * GROUP * D)
    q_mine, g_mine = simple(stage_kernel, (half, half), 2)(info, queries, out_grad)
    rest, near, q_mine, g_mine = lax.optimization_barrier((payloads[1:], near, q_mine, g_mine))
    came = [(near, far)]
    came += [(send(p, ring(2)), send(p, ring(4))) for p in rest]

    dq, sums, kv_mine, kv_other = [], [], [], []
    for j in range(CHUNKS):
        *dq, own, out1, out2 = main_call(j, info, payloads[j], *came[j], q_mine, q_other, g_mine, g_other, *dq)
        if sums:
            out1, out2, dq, sums[-1] = lax.optimization_barrier((out1, out2, dq, sums[-1]))
        b2 = send(out2, ring(-4))
        b1 = send(out1, ring(-2))
        sums.append((own, b1, b2))
    d_query, token = pl.pallas_call(
        place_kernel,
        out_shape=(shape(T, 2 * CORE_HEADS * GROUP * D), shape(8, T, dtype=F32)),
        in_specs=[SMEM, VMEM, VMEM],
        out_specs=(VMEM, VMEM),
        compiler_params=pltpu.CompilerParams(vmem_limit_bytes=SMALL),
        cost_estimate=FREE,
    )(info, dq[0], send(dq[1], swap))
    half = shape(2 * HC * T, T)
    for j in range(CHUNKS):
        a, b = pl.pallas_call(
            sum_kernel,
            out_shape=(half, half),
            in_specs=[SMEM, VMEM, VMEM, VMEM, ANY],
            out_specs=(VMEM, VMEM),
            compiler_params=pltpu.CompilerParams(vmem_limit_bytes=SMALL),
            cost_estimate=FREE,
        )(info, *sums[j], token if j == CHUNKS - 1 else info)
        kv_mine.append(a)
        kv_other.append(send(b, swap))
    out = shape(T, 2 * CORE_HEADS * D)
    d_key, d_value = pl.pallas_call(
        last_kernel,
        out_shape=(out, out),
        in_specs=[SMEM] + [VMEM] * (2 * CHUNKS),
        out_specs=(VMEM, VMEM),
        compiler_params=pltpu.CompilerParams(vmem_limit_bytes=SMALL),
            cost_estimate=FREE,
    )(info, *kv_mine, *kv_other)
    return (d_query, d_key, d_value)


def solution(mesh):
    row = P(("dp", "sp"), None)
    return jax.shard_map(
        body,
        mesh=mesh,
        in_specs=(row, row, row, row, P(("dp", "sp"))),
        out_specs=(row, row, row),
        check_vma=False,
    )
```

```python
import functools

import jax
import jax.numpy as jnp
from jax import lax
from jax.experimental import pallas as pl
from jax.experimental.pallas import tpu as pltpu
from jax.sharding import PartitionSpec as P

D = 128
T = 128
GROUP = 8
NEG = -1e30
CHUNKS = 2
CORE_HEADS = 4
HC = CORE_HEADS // CHUNKS
PAY = HC * 512 + 16
SMALL = 16 * 1024 * 1024
ROWS = 128
HALF = 512
SCALE = D ** -0.5
LOG2E = 1.4426950408889634
NT = (((1,), (1,)), ((), ()))
TN = (((0,), (0,)), ((), ()))
NN = (((1,), (0,)), ((), ()))
F32 = jnp.float32
BF16 = jnp.bfloat16


def rows(start, size, step=128):
    return pl.ds(pl.multiple_of(start, step), size)


def prep_kernel(info, key_in, value_in, ids_in, mine, theirs, key, value, ids, sems):
    c = info[0]
    pairs = ((key_in, key), (value_in, value), (ids_in, ids))
    copies = [pltpu.make_async_copy(a, b, sems.at[i]) for i, (a, b) in enumerate(pairs)]
    for copy in copies:
        copy.start()
    for copy in copies:
        copy.wait()
    for out, core in ((theirs, 1 - c), (mine, c)):
        for h in range(CORE_HEADS):
            cols = rows((core * CORE_HEADS + h) * D, D)
            out[(2 * h) * T:(2 * h + 1) * T, :] = key[:, cols]
            out[(2 * h + 1) * T:(2 * h + 2) * T, :] = value[:, cols]
        out[2 * CORE_HEADS * T:, :] = jnp.broadcast_to(ids[...].astype(F32), (16, T)).astype(BF16)


def join_kernel(info, mine, other, *outs):
    c = info[0]
    for j, out in enumerate(outs):
        for ht in range(2 * HC):
            src = (j * 2 * HC + ht) * T
            out[rows(ht * 256 + c * T, T), :] = mine[src:src + T, :]
            out[rows(ht * 256 + (1 - c) * T, T), :] = other[src:src + T, :]
        a = mine[2 * CORE_HEADS * T:, :].astype(F32)
        b = other[2 * CORE_HEADS * T:, :].astype(F32)
        row = lax.broadcasted_iota(jnp.int32, (16, T), 0)
        out[HC * 512:, :] = jnp.where(row == c, a, b).astype(BF16)


def load_ids(info, idrow, kvo, kv1, kv2):
    ids = slice(HC * 512, HC * 512 + 2)
    idrow[0:2, :] = jnp.where(info[1] >= 2, kv2[ids, :].astype(F32), -1.0)
    idrow[2:4, :] = jnp.where(info[1] >= 1, kv1[ids, :].astype(F32), -1.0)
    idrow[4:6, :] = kvo[ids, :].astype(F32)


def first_id(idrow, s):
    mine = idrow[pl.ds(s + 4, 1), :]
    return jnp.max(jnp.where(lax.broadcasted_iota(jnp.int32, (1, T), 1) == 0, mine, -2.0))


def block_count(idrow, s):
    count = jnp.int32(1)
    for b in range(4):
        same = jnp.max(idrow[pl.ds(s + b, 1), :]) == first_id(idrow, s)
        count = count + same.astype(jnp.int32)
    return count


def main_kernel(chunk, info, kvo, kv1, kv2, qs, gs, own, out1, out2, ds,
                idrow, nb, bias, kwin, vwin, acc_k, acc_v, ps, es, dps):
    base = chunk * HC
    c = info[0]
    load_ids(info, idrow, kvo, kv1, kv2)
    key_at = lax.broadcasted_iota(jnp.int32, (T, T), 0)
    query_at = lax.broadcasted_iota(jnp.int32, (T, T), 1)
    for n in range(2):
        s = c if n == 0 else 1 - c
        mine = idrow[pl.ds(s + 4, 1), :]
        for b in range(5):
            keys = idrow[pl.ds(s + b, 1), :]
            same = jnp.transpose(jnp.broadcast_to(keys, (T, T))) == mine
            if b == 4:
                same = same & (key_at <= query_at)
            bias[n, b * T:(b + 1) * T, :] = jnp.where(same, 0.0, NEG)
        nb[n] = block_count(idrow, s)

    def window(h, n, off, blocks):
        width = blocks * T
        skip = 640 - width
        at = rows(off + skip, width)
        kw, vw = kwin[at, :], vwin[at, :]
        b1 = bias[n, skip:, :]
        b2 = jnp.concatenate([b1, b1], axis=1)
        row = (base + h) * 1024
        for pair in range(GROUP // 2):
            cols = slice(pair * 256, (pair + 1) * 256)
            of_pair = rows(row + pair * 256, 256)
            score = lax.dot_general(kw, qs[n, of_pair, :], NT, preferred_element_type=F32)
            dp = lax.dot_general(vw, gs[n, of_pair, :], NT, preferred_element_type=F32)
            stats = []
            for b in range(0, width, ROWS):
                x = score[b:b + ROWS] * (SCALE * LOG2E) + b2[b:b + ROWS]
                x = x.reshape(ROWS // 8, 8, 256)
                y = dp[b:b + ROWS].reshape(ROWS // 8, 8, 256)
                top = jnp.max(x, axis=0)
                e = jnp.exp2(x - top)
                stats.append((top, jnp.sum(e, axis=0), jnp.sum(e * y, axis=0)))
                es[pair % 2, b:b + ROWS, :] = e.reshape(ROWS, 256)
                dps[pair % 2, b:b + ROWS, :] = dp[b:b + ROWS]
            top = stats[0][0]
            for t, _, _ in stats[1:]:
                top = jnp.maximum(top, t)
            top = jnp.max(top, axis=0, keepdims=True)
            fs = [jnp.exp2(t - top) for t, _, _ in stats]
            total = sum(f * l for f, (_, l, _) in zip(fs, stats))
            inv = 1.0 / jnp.sum(total, axis=0, keepdims=True)
            total = sum(f * d for f, (_, _, d) in zip(fs, stats))
            delta = jnp.sum(total, axis=0, keepdims=True) * inv
            for b, f in zip(range(0, width, ROWS), fs):
                at_b = slice(b, b + ROWS)
                p = es[pair % 2, at_b, :].reshape(ROWS // 8, 8, 256) * (f * inv)
                y = dps[pair % 2, at_b, :].reshape(ROWS // 8, 8, 256)
                ps[at_b, cols] = p.reshape(ROWS, 256).astype(BF16)
                ds[h, n, skip + b:skip + b + ROWS, cols] = (p * (y - delta)).reshape(ROWS, 256).astype(BF16)
            done = (pair + 1) * 256
            if done % HALF == 0:
                part = slice(done - HALF, done)
                of_part = rows(row + done - HALF, HALF)
                acc_v[at, :] += lax.dot_general(
                    ps[0:width, part], gs[n, of_part, :], NN, preferred_element_type=F32)
                acc_k[at, :] += lax.dot_general(
                    ds[h, n, skip:, part], qs[n, of_part, :], NN, preferred_element_type=F32)

    def one_head(h, carry):
        for at, ref in ((0, kv2), (256, kv1), (512, kvo)):
            kwin[at:at + 256, :] = ref[rows(h * 512, 256), :]
            vwin[at:at + 256, :] = ref[rows(h * 512 + 256, 256), :]
        acc_k[...] = jnp.zeros_like(acc_k)
        acc_v[...] = jnp.zeros_like(acc_v)

        def half(n, carry):
            off = jnp.where(n == 0, c, 1 - c) * T
            for blocks in range(1, 6):
                @pl.when(nb[n] == blocks)
                def _():
                    window(h, n, off, blocks)
            return carry

        lax.fori_loop(0, 2, half, 0)
        for at, ref in ((0, out2), (256, out1), (512, own)):
            ref[rows(h * 512, 256), :] = (acc_k[at:at + 256, :] * SCALE).astype(ref.dtype)
            ref[rows(h * 512 + 256, 256), :] = acc_v[at:at + 256, :].astype(ref.dtype)
        return carry

    lax.fori_loop(0, HC, one_head, 0)


def query_kernel(info, *refs):
    c = info[0]
    ins, (dqo, dqr, idrow, nb, kwin, dqs) = refs[:4 * CHUNKS], refs[4 * CHUNKS:]
    load_ids(info, idrow, *ins[:3])
    for n in range(2):
        nb[n] = block_count(idrow, c if n == 0 else 1 - c)
    for j in range(CHUNKS):
        kvo, kv1, kv2, ds = ins[4 * j:4 * j + 4]

        def one_head(h, carry):
            for at, ref in ((0, kv2), (256, kv1), (512, kvo)):
                kwin[at:at + 256, :] = ref[rows(h * 512, 256), :]
            col = (j * HC + h) * (GROUP * D)
            for n, out in enumerate((dqo, dqr)):
                off = (c if n == 0 else 1 - c) * T
                for blocks in range(1, 6):
                    @pl.when(nb[n] == blocks)
                    def _():
                        skip = 640 - blocks * T
                        kw = kwin[rows(off + skip, blocks * T), :]
                        dqs[...] = (lax.dot_general(
                            ds[h, n, skip:, :], kw, TN, preferred_element_type=F32) * SCALE
                        ).astype(BF16)
                for i in range(GROUP):
                    out[:, rows(col + i * D, D)] = dqs[i * T:(i + 1) * T, :]
            return carry

        lax.fori_loop(0, HC, one_head, 0)


def stage_kernel(info, query, grad, query_other, grad_other, qs, gs):
    start = info[0] * (CORE_HEADS * GROUP * D)
    for n, parts in enumerate(((query, grad), (query_other, grad_other))):
        for part, out in zip(parts, (qs, gs)):
            for i in range(CORE_HEADS * GROUP):
                out[n, i * T:(i + 1) * T, :] = part[:, rows(start + i * D, D)]


def place_kernel(info, mine, other, after, out, token):
    c = info[0]
    width = CORE_HEADS * GROUP * D
    for part, core in ((mine, c), (other, 1 - c)):
        for i in range(0, width, D):
            out[:, rows(core * width + i, D)] = part[:, i:i + D]
    token[...] = jnp.zeros_like(token)


def sum_kernel(info, own, b1, b2, mine, theirs):
    c = info[0]
    for out, core in ((mine, c), (theirs, 1 - c)):
        for ht in range(2 * HC):
            at = rows(ht * 256 + core * T, T)
            out[ht * T:(ht + 1) * T, :] = (
                own[at, :] + b1[at, :].astype(F32) + b2[at, :].astype(F32)).astype(BF16)


def last_kernel(info, *refs):
    c = info[0]
    mine, other, (key, value) = refs[:CHUNKS], refs[CHUNKS:2 * CHUNKS], refs[2 * CHUNKS + 1:]
    for part, core in ((mine, c), (other, 1 - c)):
        for j in range(CHUNKS):
            for h in range(HC):
                cols = rows((core * CORE_HEADS + j * HC + h) * D, D)
                key[:, cols] = part[j][(2 * h) * T:(2 * h + 1) * T, :]
                value[:, cols] = part[j][(2 * h + 1) * T:(2 * h + 2) * T, :]


def shape(*dims, dtype=BF16):
    return jax.ShapeDtypeStruct(dims, dtype)


SMEM = pl.BlockSpec(memory_space=pltpu.SMEM)
ANY = pl.BlockSpec(memory_space=pl.ANY)
HBM = pl.BlockSpec(memory_space=pltpu.HBM)
FREE = pl.CostEstimate(flops=0, bytes_accessed=0, transcendentals=0)
MID = pl.CostEstimate(flops=2 * 10 ** 10, bytes_accessed=0, transcendentals=0)
LONG = pl.CostEstimate(flops=10 ** 11, bytes_accessed=10 ** 8, transcendentals=0)
VMEM = pl.BlockSpec(memory_space=pltpu.VMEM)


def simple(kernel, outs, count, flops=0):
    return pl.pallas_call(
        kernel,
        out_shape=outs,
        in_specs=[SMEM] + [VMEM] * count,
        out_specs=tuple(VMEM for _ in outs),
        compiler_params=pltpu.CompilerParams(vmem_limit_bytes=SMALL),
            cost_estimate=FREE,
    )


def main_call(chunk, info, payload, r1, r2, qs, gs):
    return pl.pallas_call(
        functools.partial(main_kernel, chunk),
        in_specs=[SMEM] + [VMEM] * 5,
        out_specs=[VMEM] * 4,
        scratch_shapes=[
            pltpu.VMEM((8, T), F32),
            pltpu.SMEM((2,), jnp.int32),
            pltpu.VMEM((2, 640, T), F32),
            pltpu.VMEM((768, D), BF16),
            pltpu.VMEM((768, D), BF16),
            pltpu.VMEM((768, D), F32),
            pltpu.VMEM((768, D), F32),
            pltpu.VMEM((640, 1024), BF16),
            pltpu.VMEM((2, 640, 256), F32),
            pltpu.VMEM((2, 640, 256), F32),
        ],
        out_shape=[
            shape(HC * 512, T, dtype=F32),
            shape(HC * 512, T),
            shape(HC * 512, T),
            shape(HC, 2, 640, 1024),
        ],
        compiler_params=pltpu.CompilerParams(vmem_limit_bytes=24 * 1024 * 1024),
        cost_estimate=LONG,
    )(info, payload, r1, r2, qs, gs)


def body(queries, key_heads, value_heads, out_grad, segment_ids):
    devices = lax.axis_size("sp")
    me = lax.axis_index("sp")
    c, k = me % 2, me // 2
    info = jnp.stack([c, k]).astype(jnp.int32)
    swap = [(i, i ^ 1) for i in range(devices)]

    def ring(by):
        return [(i, (i + by) % devices) for i in range(devices)]

    def send(x, perm):
        return lax.ppermute(x, "sp", perm)

    side = shape(2 * CORE_HEADS * T + 16, T)
    kv_in = pltpu.VMEM((T, 2 * CORE_HEADS * D), BF16)
    mine, theirs = pl.pallas_call(
        prep_kernel,
        out_shape=(side, side),
        in_specs=[SMEM, HBM, HBM, HBM],
        out_specs=(VMEM, VMEM),
        scratch_shapes=[
            kv_in, kv_in, pltpu.VMEM((1, T), jnp.int32), pltpu.SemaphoreType.DMA((3,))],
        compiler_params=pltpu.CompilerParams(vmem_limit_bytes=SMALL),
        cost_estimate=FREE,
    )(info, key_heads, value_heads, segment_ids.reshape(1, T))
    other = send(theirs, swap)
    q_late, g_late, other = lax.optimization_barrier((queries, out_grad, other))
    q_other, g_other = send(q_late, swap), send(g_late, swap)
    payloads = simple(join_kernel, (shape(PAY, T),) * CHUNKS, 2)(info, mine, other)
    near, far = send(payloads[0], ring(2)), send(payloads[0], ring(4))
    stacked = shape(2, CORE_HEADS * GROUP * T, D)
    qs, gs = simple(stage_kernel, (stacked, stacked), 4)(info, queries, out_grad, q_other, g_other)
    rest, qs, gs = lax.optimization_barrier((payloads[1:], qs, gs))
    came = [(near, far)]
    came += [(send(p, ring(2)), send(p, ring(4))) for p in rest]

    sums, score_grads, kv_mine, kv_other = [], [], [], []
    for j in range(CHUNKS):
        own, out1, out2, ds = main_call(j, info, payloads[j], *came[j], qs, gs)
        if sums:
            own_a, near_a, far_a = sums[-1]
            out1, out2, ds, near_a = lax.optimization_barrier((out1, out2, ds, near_a))
            sums[-1] = own_a, near_a, far_a
        b2 = send(out2, ring(-4))
        b1 = send(out1, ring(-2))
        sums.append((own, b1, b2))
        score_grads += [payloads[j], *came[j], ds]
    half = shape(T, CORE_HEADS * GROUP * D)
    dq_mine, dq_send = pl.pallas_call(
        query_kernel,
        out_shape=(half, half),
        in_specs=[SMEM] + [VMEM] * (4 * CHUNKS),
        out_specs=(VMEM, VMEM),
        scratch_shapes=[
            pltpu.VMEM((8, T), F32),
            pltpu.SMEM((2,), jnp.int32),
            pltpu.VMEM((768, D), BF16),
            pltpu.VMEM((1024, D), BF16),
        ],
        compiler_params=pltpu.CompilerParams(vmem_limit_bytes=SMALL),
        cost_estimate=LONG,
    )(info, *score_grads)
    dq_other = send(dq_send, swap)
    half = shape(2 * HC * T, T)
    for j in range(CHUNKS):
        a, b = pl.pallas_call(
            sum_kernel,
            out_shape=(half, half),
            in_specs=[SMEM, VMEM, VMEM, VMEM],
            out_specs=(VMEM, VMEM),
            compiler_params=pltpu.CompilerParams(vmem_limit_bytes=SMALL),
            cost_estimate=MID if j == CHUNKS - 1 else FREE,
        )(info, *sums[j])
        kv_mine.append(a)
        kv_other.append(send(b, swap))
    d_query, token = pl.pallas_call(
        place_kernel,
        out_shape=(shape(T, 2 * CORE_HEADS * GROUP * D), shape(8, T, dtype=F32)),
        in_specs=[SMEM, VMEM, VMEM, ANY],
        out_specs=(VMEM, VMEM),
        compiler_params=pltpu.CompilerParams(vmem_limit_bytes=SMALL),
        cost_estimate=FREE,
    )(info, dq_mine, dq_other, kv_mine[-1])
    out = shape(T, 2 * CORE_HEADS * D)
    d_key, d_value = pl.pallas_call(
        last_kernel,
        out_shape=(out, out),
        in_specs=[SMEM] + [VMEM] * (2 * CHUNKS) + [ANY],
        out_specs=(VMEM, VMEM),
        compiler_params=pltpu.CompilerParams(vmem_limit_bytes=SMALL),
            cost_estimate=FREE,
    )(info, *kv_mine, *kv_other, token)
    return (d_query, d_key, d_value)


def solution(mesh):
    row = P(("dp", "sp"), None)
    return jax.shard_map(
        body,
        mesh=mesh,
        in_specs=(row, row, row, row, P(("dp", "sp"))),
        out_specs=(row, row, row),
        check_vma=False,
    )
```

```python
import functools

import jax
import jax.numpy as jnp
from jax import lax
from jax.experimental import pallas as pl
from jax.experimental.pallas import tpu as pltpu
from jax.sharding import PartitionSpec as P

D = 128
T = 128
GROUP = 8
NEG = -1e30
CHUNKS = 2
CORE_HEADS = 4
HC = CORE_HEADS // CHUNKS
PAY = HC * 512 + 16
SMALL = 16 * 1024 * 1024
BIG = 60 * 1024 * 1024
ROWS = 128
HALF = 512
SCALE = D ** -0.5
LOG2E = 1.4426950408889634
NT = (((1,), (1,)), ((), ()))
TN = (((0,), (0,)), ((), ()))
NN = (((1,), (0,)), ((), ()))
F32 = jnp.float32
BF16 = jnp.bfloat16


def rows(start, size, step=128):
    return pl.ds(pl.multiple_of(start, step), size)


def prep_kernel(key_in, value_in, ids_in, mine, theirs, key, value, ids, sems):
    c = lax.axis_index("sp") % 2
    pairs = ((key_in, key), (value_in, value), (ids_in, ids))
    copies = [pltpu.make_async_copy(a, b, sems.at[i]) for i, (a, b) in enumerate(pairs)]
    for copy in copies:
        copy.start()
    for copy in copies:
        copy.wait()
    for out, core in ((theirs, 1 - c), (mine, c)):
        for h in range(CORE_HEADS):
            cols = rows((core * CORE_HEADS + h) * D, D)
            out[(2 * h) * T:(2 * h + 1) * T, :] = key[:, cols]
            out[(2 * h + 1) * T:(2 * h + 2) * T, :] = value[:, cols]
        out[2 * CORE_HEADS * T:, :] = jnp.broadcast_to(ids[...].astype(F32), (16, T)).astype(BF16)


def join_kernel(info, mine, other, *outs):
    c = info[0]
    for j, out in enumerate(outs):
        for ht in range(2 * HC):
            src = (j * 2 * HC + ht) * T
            out[rows(ht * 256 + c * T, T), :] = mine[src:src + T, :]
            out[rows(ht * 256 + (1 - c) * T, T), :] = other[src:src + T, :]
        a = mine[2 * CORE_HEADS * T:, :].astype(F32)
        b = other[2 * CORE_HEADS * T:, :].astype(F32)
        row = lax.broadcasted_iota(jnp.int32, (16, T), 0)
        out[HC * 512:, :] = jnp.where(row == c, a, b).astype(BF16)


def load_ids(info, idrow, kvo, kv1, kv2):
    ids = slice(HC * 512, HC * 512 + 2)
    idrow[0:2, :] = jnp.where(info[1] >= 2, kv2[ids, :].astype(F32), -1.0)
    idrow[2:4, :] = jnp.where(info[1] >= 1, kv1[ids, :].astype(F32), -1.0)
    idrow[4:6, :] = kvo[ids, :].astype(F32)


def first_id(idrow, s):
    mine = idrow[pl.ds(s + 4, 1), :]
    return jnp.max(jnp.where(lax.broadcasted_iota(jnp.int32, (1, T), 1) == 0, mine, -2.0))


def block_count(idrow, s):
    count = jnp.int32(1)
    for b in range(4):
        same = jnp.max(idrow[pl.ds(s + b, 1), :]) == first_id(idrow, s)
        count = count + same.astype(jnp.int32)
    return count


def main_kernel(chunk, info, kvo, kv1, kv2, qs, gs, own, out1, out2, ds,
                idrow, nb, bias, kwin, vwin, acc_k, acc_v, ps, es, dps):
    base = chunk * HC
    c = info[0]
    load_ids(info, idrow, kvo, kv1, kv2)
    key_at = lax.broadcasted_iota(jnp.int32, (T, T), 0)
    query_at = lax.broadcasted_iota(jnp.int32, (T, T), 1)
    for n in range(2):
        s = c if n == 0 else 1 - c
        mine = idrow[pl.ds(s + 4, 1), :]
        for b in range(5):
            keys = idrow[pl.ds(s + b, 1), :]
            same = jnp.transpose(jnp.broadcast_to(keys, (T, T))) == mine
            if b == 4:
                same = same & (key_at <= query_at)
            bias[n, b * T:(b + 1) * T, :] = jnp.where(same, 0.0, NEG)
        nb[n] = block_count(idrow, s)

    def window(h, n, off, blocks):
        width = blocks * T
        skip = 640 - width
        at = rows(off + skip, width)
        kw, vw = kwin[at, :], vwin[at, :]
        b1 = bias[n, skip:, :]
        b2 = jnp.concatenate([b1, b1], axis=1)
        row = (base + h) * 1024
        for pair in range(GROUP // 2):
            cols = slice(pair * 256, (pair + 1) * 256)
            of_pair = rows(row + pair * 256, 256)
            score = lax.dot_general(kw, qs[n, of_pair, :], NT, preferred_element_type=F32)
            dp = lax.dot_general(vw, gs[n, of_pair, :], NT, preferred_element_type=F32)
            stats = []
            for b in range(0, width, ROWS):
                x = score[b:b + ROWS] * (SCALE * LOG2E) + b2[b:b + ROWS]
                x = x.reshape(ROWS // 8, 8, 256)
                y = dp[b:b + ROWS].reshape(ROWS // 8, 8, 256)
                top = jnp.max(x, axis=0)
                e = jnp.exp2(x - top)
                stats.append((top, jnp.sum(e, axis=0), jnp.sum(e * y, axis=0)))
                es[pair % 2, b:b + ROWS, :] = e.reshape(ROWS, 256)
                dps[pair % 2, b:b + ROWS, :] = dp[b:b + ROWS]
            top = stats[0][0]
            for t, _, _ in stats[1:]:
                top = jnp.maximum(top, t)
            top = jnp.max(top, axis=0, keepdims=True)
            fs = [jnp.exp2(t - top) for t, _, _ in stats]
            total = sum(f * l for f, (_, l, _) in zip(fs, stats))
            inv = 1.0 / jnp.sum(total, axis=0, keepdims=True)
            total = sum(f * d for f, (_, _, d) in zip(fs, stats))
            delta = jnp.sum(total, axis=0, keepdims=True) * inv
            for b, f in zip(range(0, width, ROWS), fs):
                at_b = slice(b, b + ROWS)
                p = es[pair % 2, at_b, :].reshape(ROWS // 8, 8, 256) * (f * inv)
                y = dps[pair % 2, at_b, :].reshape(ROWS // 8, 8, 256)
                ps[at_b, cols] = p.reshape(ROWS, 256).astype(BF16)
                ds[h, n, skip + b:skip + b + ROWS, cols] = (p * (y - delta)).reshape(ROWS, 256).astype(BF16)
            done = (pair + 1) * 256
            if done % HALF == 0:
                part = slice(done - HALF, done)
                of_part = rows(row + done - HALF, HALF)
                acc_v[at, :] += lax.dot_general(
                    ps[0:width, part], gs[n, of_part, :], NN, preferred_element_type=F32)
                acc_k[at, :] += lax.dot_general(
                    ds[h, n, skip:, part], qs[n, of_part, :], NN, preferred_element_type=F32)

    def one_head(h, carry):
        for at, ref in ((0, kv2), (256, kv1), (512, kvo)):
            kwin[at:at + 256, :] = ref[rows(h * 512, 256), :]
            vwin[at:at + 256, :] = ref[rows(h * 512 + 256, 256), :]
        acc_k[...] = jnp.zeros_like(acc_k)
        acc_v[...] = jnp.zeros_like(acc_v)

        def half(n, carry):
            off = jnp.where(n == 0, c, 1 - c) * T
            for blocks in range(1, 6):
                @pl.when(nb[n] == blocks)
                def _():
                    window(h, n, off, blocks)
            return carry

        lax.fori_loop(0, 2, half, 0)
        for at, ref in ((0, out2), (256, out1), (512, own)):
            ref[rows(h * 512, 256), :] = (acc_k[at:at + 256, :] * SCALE).astype(ref.dtype)
            ref[rows(h * 512 + 256, 256), :] = acc_v[at:at + 256, :].astype(ref.dtype)
        return carry

    lax.fori_loop(0, HC, one_head, 0)


def query_kernel(info, *refs):
    c = info[0]
    ins, (dqo, dqr, idrow, nb, kwin, dqs) = refs[:4 * CHUNKS], refs[4 * CHUNKS:]
    load_ids(info, idrow, *ins[:3])
    for n in range(2):
        nb[n] = block_count(idrow, c if n == 0 else 1 - c)
    for j in range(CHUNKS):
        kvo, kv1, kv2, ds = ins[4 * j:4 * j + 4]

        def one_head(h, carry):
            for at, ref in ((0, kv2), (256, kv1), (512, kvo)):
                kwin[at:at + 256, :] = ref[rows(h * 512, 256), :]
            col = (j * HC + h) * (GROUP * D)
            for n, out in enumerate((dqo, dqr)):
                off = (c if n == 0 else 1 - c) * T
                for blocks in range(1, 6):
                    @pl.when(nb[n] == blocks)
                    def _():
                        skip = 640 - blocks * T
                        kw = kwin[rows(off + skip, blocks * T), :]
                        dqs[...] = (lax.dot_general(
                            ds[h, n, skip:, :], kw, TN, preferred_element_type=F32) * SCALE
                        ).astype(BF16)
                for i in range(GROUP):
                    out[:, rows(col + i * D, D)] = dqs[i * T:(i + 1) * T, :]
            return carry

        lax.fori_loop(0, HC, one_head, 0)


def stage_kernel(info, query, grad, query_other, grad_other, qs, gs):
    start = info[0] * (CORE_HEADS * GROUP * D)
    for n, parts in enumerate(((query, grad), (query_other, grad_other))):
        for part, out in zip(parts, (qs, gs)):
            for i in range(CORE_HEADS * GROUP):
                out[n, i * T:(i + 1) * T, :] = part[:, rows(start + i * D, D)]


def place_kernel(info, part, *refs):
    out, token = refs[-2:]
    out[...] = part[...]
    token[...] = jnp.zeros_like(token)


def sum_kernel(info, own, b1, b2, after, mine, theirs):
    c = info[0]
    for out, core in ((mine, c), (theirs, 1 - c)):
        for ht in range(2 * HC):
            at = rows(ht * 256 + core * T, T)
            out[ht * T:(ht + 1) * T, :] = (
                own[at, :] + b1[at, :].astype(F32) + b2[at, :].astype(F32)).astype(BF16)


def last_kernel(info, *refs):
    c = info[0]
    mine, other, (key, value) = refs[:CHUNKS], refs[CHUNKS:2 * CHUNKS], refs[2 * CHUNKS + 1:]
    for part, core in ((mine, c), (other, 1 - c)):
        for j in range(CHUNKS):
            for h in range(HC):
                cols = rows((core * CORE_HEADS + j * HC + h) * D, D)
                key[:, cols] = part[j][(2 * h) * T:(2 * h + 1) * T, :]
                value[:, cols] = part[j][(2 * h + 1) * T:(2 * h + 2) * T, :]


def shape(*dims, dtype=BF16):
    return jax.ShapeDtypeStruct(dims, dtype)


SMEM = pl.BlockSpec(memory_space=pltpu.SMEM)
ANY = pl.BlockSpec(memory_space=pl.ANY)
HBM = pl.BlockSpec(memory_space=pltpu.HBM)
FREE = pl.CostEstimate(flops=0, bytes_accessed=0, transcendentals=0)
MID = pl.CostEstimate(flops=2 * 10 ** 10, bytes_accessed=0, transcendentals=0)
LONG = pl.CostEstimate(flops=10 ** 11, bytes_accessed=10 ** 8, transcendentals=0)
VMEM = pl.BlockSpec(memory_space=pltpu.VMEM)


def simple(kernel, outs, count, flops=0):
    return pl.pallas_call(
        kernel,
        out_shape=outs,
        in_specs=[SMEM] + [VMEM] * count,
        out_specs=tuple(VMEM for _ in outs),
        compiler_params=pltpu.CompilerParams(vmem_limit_bytes=SMALL),
            cost_estimate=FREE,
    )


def main_call(chunk, info, payload, r1, r2, qs, gs):
    return pl.pallas_call(
        functools.partial(main_kernel, chunk),
        in_specs=[SMEM] + [VMEM] * 5,
        out_specs=[VMEM] * 4,
        scratch_shapes=[
            pltpu.VMEM((8, T), F32),
            pltpu.SMEM((2,), jnp.int32),
            pltpu.VMEM((2, 640, T), F32),
            pltpu.VMEM((768, D), BF16),
            pltpu.VMEM((768, D), BF16),
            pltpu.VMEM((768, D), F32),
            pltpu.VMEM((768, D), F32),
            pltpu.VMEM((640, 1024), BF16),
            pltpu.VMEM((2, 640, 256), F32),
            pltpu.VMEM((2, 640, 256), F32),
        ],
        out_shape=[
            shape(HC * 512, T, dtype=F32),
            shape(HC * 512, T),
            shape(HC * 512, T),
            shape(HC, 2, 640, 1024),
        ],
        compiler_params=pltpu.CompilerParams(vmem_limit_bytes=24 * 1024 * 1024),
        cost_estimate=LONG,
    )(info, payload, r1, r2, qs, gs)


def body(queries, key_heads, value_heads, out_grad, segment_ids):
    devices = lax.axis_size("sp")
    me = lax.axis_index("sp")
    c, k = me % 2, me // 2
    info = jnp.stack([c, k, 1 - c]).astype(jnp.int32)
    swap = [(i, i ^ 1) for i in range(devices)]

    def ring(by):
        return [(i, (i + by) % devices) for i in range(devices)]

    def send(x, perm):
        return lax.ppermute(x, "sp", perm)

    side = shape(2 * CORE_HEADS * T + 16, T)
    kv_in = pltpu.VMEM((T, 2 * CORE_HEADS * D), BF16)
    mine, theirs = pl.pallas_call(
        prep_kernel,
        out_shape=(pltpu.VMEM(side.shape, BF16),) * 2,
        in_specs=[HBM, HBM, HBM],
        out_specs=(VMEM, VMEM),
        scratch_shapes=[
            kv_in, kv_in, pltpu.VMEM((1, T), jnp.int32), pltpu.SemaphoreType.DMA((3,))],
        compiler_params=pltpu.CompilerParams(vmem_limit_bytes=BIG),
        cost_estimate=FREE,
    )(key_heads, value_heads, segment_ids.reshape(1, T))
    other = send(theirs, swap)
    q_late, g_late, other = lax.optimization_barrier((queries, out_grad, other))
    q_other, g_other = send(q_late, swap), send(g_late, swap)
    payloads = simple(join_kernel, (shape(PAY, T),) * CHUNKS, 2)(info, mine, other)
    near, far = send(payloads[0], ring(2)), send(payloads[0], ring(4))
    stacked = shape(2, CORE_HEADS * GROUP * T, D)
    qs, gs = simple(stage_kernel, (stacked, stacked), 4)(info, queries, out_grad, q_other, g_other)
    rest, qs, gs = lax.optimization_barrier((payloads[1:], qs, gs))
    came = [(near, far)]
    came += [(send(p, ring(2)), send(p, ring(4))) for p in rest]

    sums, score_grads, kv_mine, kv_other = [], [], [], []
    for j in range(CHUNKS):
        own, out1, out2, ds = main_call(j, info, payloads[j], *came[j], qs, gs)
        if sums:
            own_a, near_a, far_a = sums[-1]
            out1, out2, ds, near_a = lax.optimization_barrier((out1, out2, ds, near_a))
            sums[-1] = own_a, near_a, far_a
        b2 = send(out2, ring(-4))
        b1 = send(out1, ring(-2))
        sums.append((own, b1, b2))
        score_grads += [payloads[j], *came[j], ds]
    half = shape(T, CORE_HEADS * GROUP * D)
    dq_mine, dq_send = pl.pallas_call(
        query_kernel,
        out_shape=(half, half),
        in_specs=[SMEM] + [VMEM] * (4 * CHUNKS),
        out_specs=(VMEM, VMEM),
        scratch_shapes=[
            pltpu.VMEM((8, T), F32),
            pltpu.SMEM((2,), jnp.int32),
            pltpu.VMEM((768, D), BF16),
            pltpu.VMEM((1024, D), BF16),
        ],
        compiler_params=pltpu.CompilerParams(vmem_limit_bytes=SMALL),
        cost_estimate=LONG,
    )(info, *score_grads)
    dq_other = send(dq_send, swap)
    def place(core, part, after, *partial):
        return pl.pallas_call(
            place_kernel,
            grid_spec=pltpu.PrefetchScalarGridSpec(
                num_scalar_prefetch=1,
                grid=(1,),
                in_specs=[VMEM] + [ANY] * (1 + len(partial)),
                out_specs=[
                    pl.BlockSpec((T, CORE_HEADS * GROUP * D), lambda i, info: (0, info[core])),
                    pl.BlockSpec((8, T), lambda i, info: (0, 0)),
                ],
            ),
            out_shape=(shape(T, 2 * CORE_HEADS * GROUP * D), shape(8, T, dtype=F32)),
            input_output_aliases={3: 0} if partial else {},
            compiler_params=pltpu.CompilerParams(vmem_limit_bytes=SMALL),
            cost_estimate=FREE,
        )(info, part, after, *partial)

    d_query, token = place(0, dq_mine, info)
    half = shape(2 * HC * T, T)
    for j in range(CHUNKS):
        a, b = pl.pallas_call(
            sum_kernel,
            out_shape=(half, half),
            in_specs=[SMEM, VMEM, VMEM, VMEM, ANY],
            out_specs=(VMEM, VMEM),
            compiler_params=pltpu.CompilerParams(vmem_limit_bytes=SMALL),
            cost_estimate=MID if j == CHUNKS - 1 else FREE,
        )(info, *sums[j], token if j == CHUNKS - 1 else info)
        kv_mine.append(a)
        kv_other.append(send(b, swap))
    d_query, token = place(2, dq_other, kv_mine[-1], d_query)
    out = shape(T, 2 * CORE_HEADS * D)
    d_key, d_value = pl.pallas_call(
        last_kernel,
        out_shape=(out, out),
        in_specs=[SMEM] + [VMEM] * (2 * CHUNKS) + [ANY],
        out_specs=(VMEM, VMEM),
        compiler_params=pltpu.CompilerParams(vmem_limit_bytes=SMALL),
            cost_estimate=FREE,
    )(info, *kv_mine, *kv_other, token)
    return (d_query, d_key, d_value)


def solution(mesh):
    row = P(("dp", "sp"), None)
    return jax.shard_map(
        body,
        mesh=mesh,
        in_specs=(row, row, row, row, P(("dp", "sp"))),
        out_specs=(row, row, row),
        check_vma=False,
    )
```

```python
import functools

import jax
import jax.numpy as jnp
from jax import lax
from jax.experimental import pallas as pl
from jax.experimental.pallas import tpu as pltpu
from jax.sharding import PartitionSpec as P

D = 128
T = 128
GROUP = 8
NEG = -1e30
CHUNKS = 2
CORE_HEADS = 4
HC = CORE_HEADS // CHUNKS
PAY = HC * 512 + 16
SMALL = 16 * 1024 * 1024
BIG = 60 * 1024 * 1024
ROWS = 64
HALF = 512
SCALE = D ** -0.5
LOG2E = 1.4426950408889634
NT = (((1,), (1,)), ((), ()))
TN = (((0,), (0,)), ((), ()))
NN = (((1,), (0,)), ((), ()))
F32 = jnp.float32
BF16 = jnp.bfloat16


def rows(start, size, step=128):
    return pl.ds(pl.multiple_of(start, step), size)


def prep_kernel(key_in, value_in, ids_in, mine, theirs, key, value, ids, sems):
    c = lax.axis_index("sp") % 2
    pairs = ((key_in, key), (value_in, value), (ids_in, ids))
    copies = [pltpu.make_async_copy(a, b, sems.at[i]) for i, (a, b) in enumerate(pairs)]
    for copy in copies:
        copy.start()
    for copy in copies:
        copy.wait()
    for out, core in ((theirs, 1 - c), (mine, c)):
        for h in range(CORE_HEADS):
            cols = rows((core * CORE_HEADS + h) * D, D)
            out[(2 * h) * T:(2 * h + 1) * T, :] = key[:, cols]
            out[(2 * h + 1) * T:(2 * h + 2) * T, :] = value[:, cols]
        out[2 * CORE_HEADS * T:, :] = jnp.broadcast_to(ids[...].astype(F32), (16, T)).astype(BF16)


def join_kernel(info, mine, other, *outs):
    c = info[0]
    for j, out in enumerate(outs):
        for ht in range(2 * HC):
            src = (j * 2 * HC + ht) * T
            out[rows(ht * 256 + c * T, T), :] = mine[src:src + T, :]
            out[rows(ht * 256 + (1 - c) * T, T), :] = other[src:src + T, :]
        a = mine[2 * CORE_HEADS * T:, :].astype(F32)
        b = other[2 * CORE_HEADS * T:, :].astype(F32)
        row = lax.broadcasted_iota(jnp.int32, (16, T), 0)
        out[HC * 512:, :] = jnp.where(row == c, a, b).astype(BF16)


def load_ids(info, idrow, kvo, kv1, kv2):
    ids = slice(HC * 512, HC * 512 + 2)
    idrow[0:2, :] = jnp.where(info[1] >= 2, kv2[ids, :].astype(F32), -1.0)
    idrow[2:4, :] = jnp.where(info[1] >= 1, kv1[ids, :].astype(F32), -1.0)
    idrow[4:6, :] = kvo[ids, :].astype(F32)


def first_id(idrow, s):
    mine = idrow[pl.ds(s + 4, 1), :]
    return jnp.max(jnp.where(lax.broadcasted_iota(jnp.int32, (1, T), 1) == 0, mine, -2.0))


def block_count(idrow, s):
    count = jnp.int32(1)
    for b in range(4):
        same = jnp.max(idrow[pl.ds(s + b, 1), :]) == first_id(idrow, s)
        count = count + same.astype(jnp.int32)
    return count


def main_kernel(chunk, info, kvo, kv1, kv2, qs, gs, own, out1, out2, ds,
                idrow, nb, bias, kwin, vwin, acc_k, acc_v, ps, es, dps):
    base = chunk * HC
    c = info[0]
    load_ids(info, idrow, kvo, kv1, kv2)
    key_at = lax.broadcasted_iota(jnp.int32, (T, T), 0)
    query_at = lax.broadcasted_iota(jnp.int32, (T, T), 1)
    for n in range(2):
        s = c if n == 0 else 1 - c
        mine = idrow[pl.ds(s + 4, 1), :]
        for b in range(5):
            keys = idrow[pl.ds(s + b, 1), :]
            same = jnp.transpose(jnp.broadcast_to(keys, (T, T))) == mine
            if b == 4:
                same = same & (key_at <= query_at)
            bias[n, b * T:(b + 1) * T, :] = jnp.where(same, 0.0, NEG)
        nb[n] = block_count(idrow, s)

    def window(h, n, off, blocks):
        width = blocks * T
        skip = 640 - width
        at = rows(off + skip, width)
        kw, vw = kwin[at, :], vwin[at, :]
        b1 = bias[n, skip:, :]
        b2 = jnp.concatenate([b1, b1], axis=1)
        row = (base + h) * 1024
        for pair in range(GROUP // 2):
            cols = slice(pair * 256, (pair + 1) * 256)
            of_pair = rows(row + pair * 256, 256)
            score = lax.dot_general(kw, qs[n, of_pair, :], NT, preferred_element_type=F32)
            dp = lax.dot_general(vw, gs[n, of_pair, :], NT, preferred_element_type=F32)
            stats = []
            for b in range(0, width, ROWS):
                x = score[b:b + ROWS] * (SCALE * LOG2E) + b2[b:b + ROWS]
                x = x.reshape(ROWS // 8, 8, 256)
                y = dp[b:b + ROWS].reshape(ROWS // 8, 8, 256)
                top = jnp.max(x, axis=0)
                e = jnp.exp2(x - top)
                stats.append((top, jnp.sum(e, axis=0), jnp.sum(e * y, axis=0)))
                es[pair % 2, b:b + ROWS, :] = e.reshape(ROWS, 256)
                dps[pair % 2, b:b + ROWS, :] = dp[b:b + ROWS]
            top = stats[0][0]
            for t, _, _ in stats[1:]:
                top = jnp.maximum(top, t)
            top = jnp.max(top, axis=0, keepdims=True)
            fs = [jnp.exp2(t - top) for t, _, _ in stats]
            total = sum(f * l for f, (_, l, _) in zip(fs, stats))
            inv = 1.0 / jnp.sum(total, axis=0, keepdims=True)
            total = sum(f * d for f, (_, _, d) in zip(fs, stats))
            delta = jnp.sum(total, axis=0, keepdims=True) * inv
            for b, f in zip(range(0, width, ROWS), fs):
                at_b = slice(b, b + ROWS)
                p = es[pair % 2, at_b, :].reshape(ROWS // 8, 8, 256) * (f * inv)
                y = dps[pair % 2, at_b, :].reshape(ROWS // 8, 8, 256)
                ps[at_b, cols] = p.reshape(ROWS, 256).astype(BF16)
                ds[h, n, skip + b:skip + b + ROWS, cols] = (p * (y - delta)).reshape(ROWS, 256).astype(BF16)
            done = (pair + 1) * 256
            if done % HALF == 0:
                part = slice(done - HALF, done)
                of_part = rows(row + done - HALF, HALF)
                acc_v[at, :] += lax.dot_general(
                    ps[0:width, part], gs[n, of_part, :], NN, preferred_element_type=F32)
                acc_k[at, :] += lax.dot_general(
                    ds[h, n, skip:, part], qs[n, of_part, :], NN, preferred_element_type=F32)

    def one_head(h, carry):
        for at, ref in ((0, kv2), (256, kv1), (512, kvo)):
            kwin[at:at + 256, :] = ref[rows(h * 512, 256), :]
            vwin[at:at + 256, :] = ref[rows(h * 512 + 256, 256), :]
        acc_k[...] = jnp.zeros_like(acc_k)
        acc_v[...] = jnp.zeros_like(acc_v)

        def half(n, carry):
            off = jnp.where(n == 0, c, 1 - c) * T
            for blocks in range(1, 6):
                @pl.when(nb[n] == blocks)
                def _():
                    window(h, n, off, blocks)
            return carry

        lax.fori_loop(0, 2, half, 0)
        for at, ref in ((0, out2), (256, out1), (512, own)):
            ref[rows(h * 512, 256), :] = (acc_k[at:at + 256, :] * SCALE).astype(ref.dtype)
            ref[rows(h * 512 + 256, 256), :] = acc_v[at:at + 256, :].astype(ref.dtype)
        return carry

    lax.fori_loop(0, HC, one_head, 0)


def query_kernel(info, *refs):
    c = info[0]
    ins, (dqo, dqr, idrow, nb, kwin, dqs) = refs[:4 * CHUNKS], refs[4 * CHUNKS:]
    load_ids(info, idrow, *ins[:3])
    for n in range(2):
        nb[n] = block_count(idrow, c if n == 0 else 1 - c)
    for j in range(CHUNKS):
        kvo, kv1, kv2, ds = ins[4 * j:4 * j + 4]

        def one_head(h, carry):
            for at, ref in ((0, kv2), (256, kv1), (512, kvo)):
                kwin[at:at + 256, :] = ref[rows(h * 512, 256), :]
            col = (j * HC + h) * (GROUP * D)
            for n, out in enumerate((dqo, dqr)):
                off = (c if n == 0 else 1 - c) * T
                for blocks in range(1, 6):
                    @pl.when(nb[n] == blocks)
                    def _():
                        skip = 640 - blocks * T
                        kw = kwin[rows(off + skip, blocks * T), :]
                        dqs[...] = (lax.dot_general(
                            ds[h, n, skip:, :], kw, TN, preferred_element_type=F32) * SCALE
                        ).astype(BF16)
                for i in range(GROUP):
                    out[:, rows(col + i * D, D)] = dqs[i * T:(i + 1) * T, :]
            return carry

        lax.fori_loop(0, HC, one_head, 0)


def stage_kernel(info, query, grad, query_other, grad_other, qs, gs):
    start = info[0] * (CORE_HEADS * GROUP * D)
    for n, parts in enumerate(((query, grad), (query_other, grad_other))):
        for part, out in zip(parts, (qs, gs)):
            for i in range(CORE_HEADS * GROUP):
                out[n, i * T:(i + 1) * T, :] = part[:, rows(start + i * D, D)]


def place_kernel(info, part, *refs):
    out, token = refs[-2:]
    out[...] = part[...]
    token[...] = jnp.zeros_like(token)


def sum_kernel(info, own, b1, b2, after, mine, theirs):
    c = info[0]
    for out, core in ((mine, c), (theirs, 1 - c)):
        for ht in range(2 * HC):
            at = rows(ht * 256 + core * T, T)
            out[ht * T:(ht + 1) * T, :] = (
                own[at, :] + b1[at, :].astype(F32) + b2[at, :].astype(F32)).astype(BF16)


def last_kernel(info, *refs):
    c = info[0]
    mine, other, (key, value) = refs[:CHUNKS], refs[CHUNKS:2 * CHUNKS], refs[2 * CHUNKS + 1:]
    for part, core in ((mine, c), (other, 1 - c)):
        for j in range(CHUNKS):
            for h in range(HC):
                cols = rows((core * CORE_HEADS + j * HC + h) * D, D)
                key[:, cols] = part[j][(2 * h) * T:(2 * h + 1) * T, :]
                value[:, cols] = part[j][(2 * h + 1) * T:(2 * h + 2) * T, :]


def shape(*dims, dtype=BF16):
    return jax.ShapeDtypeStruct(dims, dtype)


SMEM = pl.BlockSpec(memory_space=pltpu.SMEM)
ANY = pl.BlockSpec(memory_space=pl.ANY)
HBM = pl.BlockSpec(memory_space=pltpu.HBM)
FREE = pl.CostEstimate(flops=0, bytes_accessed=0, transcendentals=0)
MID = pl.CostEstimate(flops=2 * 10 ** 10, bytes_accessed=0, transcendentals=0)
LONG = pl.CostEstimate(flops=10 ** 11, bytes_accessed=10 ** 8, transcendentals=0)
VMEM = pl.BlockSpec(memory_space=pltpu.VMEM)


def simple(kernel, outs, count, flops=0):
    return pl.pallas_call(
        kernel,
        out_shape=outs,
        in_specs=[SMEM] + [VMEM] * count,
        out_specs=tuple(VMEM for _ in outs),
        compiler_params=pltpu.CompilerParams(vmem_limit_bytes=SMALL),
            cost_estimate=FREE,
    )


def main_call(chunk, info, payload, r1, r2, qs, gs):
    return pl.pallas_call(
        functools.partial(main_kernel, chunk),
        in_specs=[SMEM] + [VMEM] * 5,
        out_specs=[VMEM] * 4,
        scratch_shapes=[
            pltpu.VMEM((8, T), F32),
            pltpu.SMEM((2,), jnp.int32),
            pltpu.VMEM((2, 640, T), F32),
            pltpu.VMEM((768, D), BF16),
            pltpu.VMEM((768, D), BF16),
            pltpu.VMEM((768, D), F32),
            pltpu.VMEM((768, D), F32),
            pltpu.VMEM((640, 1024), BF16),
            pltpu.VMEM((2, 640, 256), F32),
            pltpu.VMEM((2, 640, 256), F32),
        ],
        out_shape=[
            shape(HC * 512, T, dtype=F32),
            shape(HC * 512, T),
            shape(HC * 512, T),
            shape(HC, 2, 640, 1024),
        ],
        compiler_params=pltpu.CompilerParams(vmem_limit_bytes=24 * 1024 * 1024),
        cost_estimate=LONG,
    )(info, payload, r1, r2, qs, gs)


def body(queries, key_heads, value_heads, out_grad, segment_ids):
    devices = lax.axis_size("sp")
    me = lax.axis_index("sp")
    c, k = me % 2, me // 2
    info = jnp.stack([c, k, 1 - c]).astype(jnp.int32)
    swap = [(i, i ^ 1) for i in range(devices)]

    def ring(by):
        return [(i, (i + by) % devices) for i in range(devices)]

    def send(x, perm):
        return lax.ppermute(x, "sp", perm)

    side = shape(2 * CORE_HEADS * T + 16, T)
    kv_in = pltpu.VMEM((T, 2 * CORE_HEADS * D), BF16)
    mine, theirs = pl.pallas_call(
        prep_kernel,
        out_shape=(pltpu.VMEM(side.shape, BF16),) * 2,
        in_specs=[HBM, HBM, HBM],
        out_specs=(VMEM, VMEM),
        scratch_shapes=[
            kv_in, kv_in, pltpu.VMEM((1, T), jnp.int32), pltpu.SemaphoreType.DMA((3,))],
        compiler_params=pltpu.CompilerParams(vmem_limit_bytes=BIG),
        cost_estimate=FREE,
    )(key_heads, value_heads, segment_ids.reshape(1, T))
    other = send(theirs, swap)
    q_late, g_late, other = lax.optimization_barrier((queries, out_grad, other))
    q_other, g_other = send(q_late, swap), send(g_late, swap)
    payloads = simple(join_kernel, (shape(PAY, T),) * CHUNKS, 2)(info, mine, other)
    near, far = send(payloads[0], ring(2)), send(payloads[0], ring(4))
    stacked = shape(2, CORE_HEADS * GROUP * T, D)
    qs, gs = simple(stage_kernel, (stacked, stacked), 4)(info, queries, out_grad, q_other, g_other)
    rest, qs, gs = lax.optimization_barrier((payloads[1:], qs, gs))
    came = [(near, far)]
    came += [(send(p, ring(2)), send(p, ring(4))) for p in rest]

    sums, score_grads, kv_mine, kv_other = [], [], [], []
    for j in range(CHUNKS):
        own, out1, out2, ds = main_call(j, info, payloads[j], *came[j], qs, gs)
        b2 = send(out2, ring(-4))
        b1 = send(out1, ring(-2))
        sums.append((own, b1, b2))
        score_grads += [payloads[j], *came[j], ds]
    half = shape(T, CORE_HEADS * GROUP * D)
    dq_mine, dq_send = pl.pallas_call(
        query_kernel,
        out_shape=(half, half),
        in_specs=[SMEM] + [VMEM] * (4 * CHUNKS),
        out_specs=(VMEM, VMEM),
        scratch_shapes=[
            pltpu.VMEM((8, T), F32),
            pltpu.SMEM((2,), jnp.int32),
            pltpu.VMEM((768, D), BF16),
            pltpu.VMEM((1024, D), BF16),
        ],
        compiler_params=pltpu.CompilerParams(vmem_limit_bytes=SMALL),
        cost_estimate=LONG,
    )(info, *score_grads)
    dq_other = send(dq_send, swap)
    def place(core, part, after, *partial):
        return pl.pallas_call(
            place_kernel,
            grid_spec=pltpu.PrefetchScalarGridSpec(
                num_scalar_prefetch=1,
                grid=(1,),
                in_specs=[VMEM] + [ANY] * (1 + len(partial)),
                out_specs=[
                    pl.BlockSpec((T, CORE_HEADS * GROUP * D), lambda i, info: (0, info[core])),
                    pl.BlockSpec((8, T), lambda i, info: (0, 0)),
                ],
            ),
            out_shape=(shape(T, 2 * CORE_HEADS * GROUP * D), shape(8, T, dtype=F32)),
            input_output_aliases={3: 0} if partial else {},
            compiler_params=pltpu.CompilerParams(vmem_limit_bytes=SMALL),
            cost_estimate=FREE,
        )(info, part, after, *partial)

    d_query, token = place(0, dq_mine, info)
    half = shape(2 * HC * T, T)
    for j in range(CHUNKS):
        a, b = pl.pallas_call(
            sum_kernel,
            out_shape=(half, half),
            in_specs=[SMEM, VMEM, VMEM, VMEM, ANY],
            out_specs=(VMEM, VMEM),
            compiler_params=pltpu.CompilerParams(vmem_limit_bytes=SMALL),
            cost_estimate=MID if j == CHUNKS - 1 else FREE,
        )(info, *sums[j], token if j == CHUNKS - 1 else sums[-1][0])
        kv_mine.append(a)
        kv_other.append(send(b, swap))
    d_query, token = place(2, dq_other, kv_mine[-1], d_query)
    out = shape(T, 2 * CORE_HEADS * D)
    d_key, d_value = pl.pallas_call(
        last_kernel,
        out_shape=(out, out),
        in_specs=[SMEM] + [VMEM] * (2 * CHUNKS) + [ANY],
        out_specs=(VMEM, VMEM),
        compiler_params=pltpu.CompilerParams(vmem_limit_bytes=SMALL),
            cost_estimate=FREE,
    )(info, *kv_mine, *kv_other, token)
    return (d_query, d_key, d_value)


def solution(mesh):
    row = P(("dp", "sp"), None)
    return jax.shard_map(
        body,
        mesh=mesh,
        in_specs=(row, row, row, row, P(("dp", "sp"))),
        out_specs=(row, row, row),
        check_vma=False,
    )
```
